256 devices in a mesh: loop: 32 (over z, x_hi, core), bcast: 8 (over y, x_lo).
Axes of the slice: x: 4 (x_hi: 2, x_lo: 2; x = x_hi * 2 + x_lo), y: 4, z: 8, core: 2. Of those that a mesh axis runs over, the one named last changes fastest.
Arguments:
- s_blocks: float32 [32, 8, 1, 10, 256, 256], P('loop', 'bcast'), may hold values from -6 to 6
- s_list: int32 [32, 8, 1, 10, 2], P('loop', 'bcast'), may hold values from 0 to 3, as said below
- x_blocks: float32 [32, 8, 12, 256, 256], P('loop', 'bcast'), may hold values from -0.09375 to 0.09375
- x_list: int32 [32, 8, 12, 2], P('loop', 'bcast'), may hold values from 0 to 4, as said below
- c_list: int32 [32, 8, 10, 2], P('loop', 'bcast'), may hold values from 0 to 3, as said below
- owner: int32 [32, 4], P('loop'), may hold values from 0 to 7, as said below
Outputs:
- product: float32 [32, 8, 10, 256, 256], P('loop', 'bcast')
The draws below stay inside these ranges and needn't reach their ends.
Inputs may be any that keep to these rules, and one draw needn't show every extreme that they name: `s_list`: positions within one list are distinct. `x_list`: positions within one list are distinct; entries with first value 4 are empty and stand after the occupied ones; some device's list has no empty entry. `c_list`: positions within one list are distinct. owner[l, s] = (s + q_l) mod 8 for a whole number q_l of each block-row group.
All inputs are finite; a program needn't handle non-finite values.
Results may differ from the reference program's by a relative error of at most 0.0003.
Values sent between devices are 32-bit elements; how exact they have to be, the bound alone decides.
A program may use at most 192 MiB of HBM per device.

```python
import jax
import jax.numpy as jnp
from jax import lax

BS = 256
RB = 3
KB = 4
CB = 4
STEPS = 4
SLOT_S = 10
SLOT_X = 12
SLOT_C = 10
STEP_DEV = 1
N_LOOP = 32
N_BCAST = 8


def draw_s_list(key, part):
    count = N_LOOP * N_BCAST * STEP_DEV
    keys = jax.random.split(jax.random.fold_in(key, 11), count)
    cells = jax.vmap(lambda one_key: jax.random.permutation(one_key, RB * KB)[:SLOT_S])(keys)
    placed = jnp.stack([cells // KB, cells % KB], -1).astype(jnp.int32)
    return placed.reshape((N_LOOP, N_BCAST, STEP_DEV, SLOT_S, 2))


def draw_x_list(key, part):
    count = N_LOOP * N_BCAST
    keys = jax.random.split(jax.random.fold_in(key, 23), count)
    cells = jax.vmap(lambda one_key: jax.random.permutation(one_key, KB * CB)[:SLOT_X])(keys)
    filled = jax.random.randint(jax.random.fold_in(key, 29), (count,), SLOT_X // 3, SLOT_X + 1)
    filled = filled.at[0].set(SLOT_X).at[1].set(SLOT_X // 3)
    used = jnp.arange(SLOT_X)[None, :] < filled[:, None]
    first = jnp.where(used, cells // CB, KB)
    placed = jnp.stack([first, cells % CB], -1).astype(jnp.int32)
    return placed.reshape((N_LOOP, N_BCAST, SLOT_X, 2))


def draw_c_list(key, part):
    count = N_LOOP * N_BCAST
    keys = jax.random.split(jax.random.fold_in(key, 37), count)
    cells = jax.vmap(lambda one_key: jax.random.permutation(one_key, RB * CB)[:SLOT_C])(keys)
    placed = jnp.stack([cells // CB, cells % CB], -1).astype(jnp.int32)
    return placed.reshape((N_LOOP, N_BCAST, SLOT_C, 2))


def draw_owner(key, part):
    rotate = jax.random.randint(jax.random.fold_in(key, 41), (N_LOOP,), 0, N_BCAST)
    rotate = rotate.at[0].set(N_BCAST - 1)
    return ((jnp.arange(STEPS)[None, :] + rotate[:, None]) % N_BCAST).astype(jnp.int32)


def levels(key, shape, shards, least, top_value):
    def one(axis_at, blocks):
        draws = jax.random.uniform(jax.random.fold_in(jax.random.fold_in(key, 6), axis_at), (blocks,), jnp.float32, least / len(shards), top_value / len(shards))
        return jnp.repeat(jnp.exp(draws), shape[axis_at] // blocks).reshape((-1,) + (1,) * (len(shape) - axis_at - 1))

    loudness = one(*shards[0])
    for cut in shards[1:]:
        loudness = loudness * one(*cut)
    return loudness


def normal_values(rng, shape, spread, limit, pieces=(), dtype=jnp.bfloat16):
    drawn = jax.random.normal(rng, shape, jnp.float32) * spread
    if len(pieces) > 0:
        drawn = levels(rng, shape, pieces, -0.22, 0.18) * drawn
    return jnp.clip(drawn, min=-limit, max=limit).astype(dtype)


def setup_inputs(seed: int = 0) -> dict:
    key_list = jax.random.split(jax.random.key(seed), 7)
    return {
        "s_blocks": normal_values(key_list[0], (N_LOOP, N_BCAST, STEP_DEV, SLOT_S, BS, BS), 1.0, 6.0, ((0, 32), (1, 8)), jnp.float32),
        "s_list": draw_s_list(jax.random.fold_in(key_list[6], 71), 0),
        "x_blocks": normal_values(key_list[2], (N_LOOP, N_BCAST, SLOT_X, BS, BS), (BS * KB * STEPS) ** -0.5, 0.09375, ((0, 32), (1, 8)), jnp.float32),
        "x_list": draw_x_list(jax.random.fold_in(key_list[6], 71), 0),
        "c_list": draw_c_list(jax.random.fold_in(key_list[6], 71), 0),
        "owner": draw_owner(jax.random.fold_in(key_list[6], 71), 0),
    }


HIGHEST = lax.Precision.HIGHEST


def densify(blocks, places, row_count, col_count):
    chosen = (places[:, 0][:, None, None] == jnp.arange(row_count)[None, :, None]) & (places[:, 1][:, None, None] == jnp.arange(col_count)[None, None, :])
    return jnp.einsum("irc,iab->rcab", chosen.astype(jnp.float32), blocks, precision=HIGHEST)


def retained(left, right, pairs):
    picked_left = left[pairs[:, 0]]
    picked_right = jnp.moveaxis(right[:, pairs[:, 1]], 1, 0)
    return jnp.einsum("jkab,jkbd->jad", picked_left, picked_right, precision=HIGHEST)


def reference(s_blocks, s_list, x_blocks, x_list, c_list, owner):
    def one_row(line):
        def one_device(column):
            total = jnp.zeros((SLOT_C, BS, BS), jnp.float32)
            pairs = c_list[line, column]
            for step in range(STEPS):
                root = owner[line, step]
                slot = step // N_BCAST
                left = densify(s_blocks[line, root, slot], s_list[line, root, slot], RB, KB)
                source = (line + step) % N_LOOP
                right = densify(x_blocks[source, column], x_list[source, column], KB, CB)
                total = total + retained(left, right, pairs)
            return total
        return lax.map(one_device, jnp.arange(N_BCAST))
    return lax.map(one_row, jnp.arange(N_LOOP))
```

```python
import jax
import jax.numpy as jnp
from jax import lax
from jax.experimental import pallas as pl
from jax.experimental.pallas import tpu as pltpu
from jax.sharding import PartitionSpec as P

RB = 3
KB = 4
CB = 4
STEPS = 4
NS = 10
NX = 12
NC = 10
NT = 4
NR = 2
HALF = NS // 2
MESH = pl.DeviceIdType.MESH
BF16 = jnp.bfloat16
F32 = jnp.float32


def kernel(meta_s, meta_v, s_hbm, x_hbm, o_hbm, *rest):
    lbufs = rest[:NT]
    (recv1, r_own, r_a, r_two, r_b, rd_hi, rd_lo, l_dense, acc, out_v, group_v, density_v,
     group_s, density_s, ss, rs, rss, rrs, ms, mr, own_sem, local_sem, out_sem) = rest[NT:]
    bs = s_hbm.shape[-1]
    tr = bs // NT
    n_loop, n_bcast = lax.axis_size("loop"), lax.axis_size("bcast")
    l, b = lax.axis_index("loop"), lax.axis_index("bcast")
    core = lax.rem(l, 2)
    hi_x = lax.rem(l // 2, 2)
    half = b // 4

    def loop_at(by):
        return (lax.rem(l + by + n_loop, n_loop), b)

    def bcast_at(by):
        return (l, lax.rem(b + by + n_bcast, n_bcast))

    def crossed(dev):
        return dev + 1 - 2 * lax.rem(dev, 2)

    def slot(dev):
        return 2 * lax.rem(dev, 4) + dev // 4

    across = (l, crossed(b))
    up, down = bcast_at(2), bcast_at(-2)
    sibling = (l + 1 - 2 * core, b)

    barrier = pltpu.get_barrier_semaphore()
    peers = [bcast_at(i) for i in range(1, 8)] + [loop_at(i) for i in (-3, -2, -1, 1, 2, 3)]
    for peer in peers:
        pl.semaphore_signal(barrier, inc=1, device_id=peer, device_id_type=MESH)
    pl.semaphore_wait(barrier, len(peers))

    def remote(src, dst, send_sem, recv_sem, dev):
        return pltpu.make_async_remote_copy(
            src_ref=src, dst_ref=dst, send_sem=send_sem, recv_sem=recv_sem, device_id=dev, device_id_type=MESH
        )

    def whole(t, dev):
        return lbufs[t].at[pl.ds(HALF * slot(dev), HALF)]

    def part(t, dev, j):
        return lbufs[t].at[pl.ds(HALF * slot(dev), HALF), pl.ds(j * (tr // 2), tr // 2)]

    left, right = down[1], up[1]

    def margin(t, kind):
        if kind == 0:
            src = s_hbm.at[pl.ds(HALF * (1 - half), HALF), pl.ds(t * tr, tr)]
            return remote(src, recv1.at[t], ss.at[t, 0], rs.at[t, 0], bcast_at(4))
        ref, dev = {
            1: (lambda: whole(t, b), across),
            2: (lambda: whole(t, b), up),
            3: (lambda: whole(t, b), down),
            4: (lambda: whole(t, across[1]), up),
            5: (lambda: whole(t, across[1]), down),
            6: (lambda: part(t, left, 0), up),
            7: (lambda: part(t, right, 1), down),
            8: (lambda: part(t, crossed(left), 0), up),
            9: (lambda: part(t, crossed(right), 1), down),
        }[kind]
        return remote(ref(), ref(), ss.at[t, kind], rs.at[t, kind], dev)

    xn = NX // NR

    def density(kind, j):
        at = pl.ds(j * xn, xn)
        dev, src, dst = {
            0: (loop_at(-2), x_hbm, r_two),
            1: ((lax.rem(l - 3 + 2 * core + n_loop, n_loop), b), x_hbm, r_a),
            2: (sibling, r_two, r_b),
        }[kind]
        return remote(src.at[at], dst.at[at], rss.at[kind, j], rrs.at[kind, j], dev)

    def relay(j):
        at = pl.ds(j * xn, xn)
        return remote(r_a.at[at], r_two.at[at], rss.at[3, j], rrs.at[0, j], loop_at(1))

    relays = jnp.logical_and(hi_x == 0, core == 1)
    direct = jnp.logical_not(jnp.logical_and(hi_x == 0, core == 0))

    def own_half(t):
        src = s_hbm.at[pl.ds(HALF * half, HALF), pl.ds(t * tr, tr)]
        return pltpu.make_async_copy(src, whole(t, b), own_sem.at[t])

    for j in range(NR):
        density(1, j).start()
    margin(0, 0).start()
    own_half(0).start()

    @pl.when(direct)
    def _():
        for j in range(NR):
            density(0, j).start()

    own_density = pltpu.make_async_copy(x_hbm, r_own, local_sem.at[0])
    own_density.start()
    for t in range(1, NT):
        margin(t, 0).start()
        own_half(t).start()

    def table(i):
        if i < 7:
            return remote(meta_v, group_v.at[b], ms.at[i], mr.at[i], bcast_at(i + 1))
        by = i - 6
        return remote(meta_v, density_v.at[by], ms.at[i], mr.at[i], loop_at(-by))

    for i in range(10):
        table(i).start()
    mine_g = pltpu.make_async_copy(meta_v, group_v.at[b], local_sem.at[1])
    mine_d = pltpu.make_async_copy(meta_v, density_v.at[0], local_sem.at[2])
    mine_g.start()
    mine_d.start()

    def split(block):
        high = block.astype(BF16)
        return high, (block - high.astype(F32)).astype(BF16)

    def spread_density(ref, j, step):
        def body(i, carry):
            k, c = i // CB, lax.rem(i, CB)
            at = density_s[step, 0, 16 + i]
            block = jnp.where(at < NX, ref[jnp.minimum(at, NX - 1)], 0.0)
            rows = pl.ds(pl.multiple_of(k * bs, bs), bs)
            high, low = split(block)
            rd_hi[j, c, rows, :] = high
            rd_lo[j, c, rows, :] = low
            return carry

        lax.fori_loop(0, KB * CB, body, 0)

    wanted = (meta_s[0, 48] == b) | (meta_s[0, 49] == b) | (meta_s[0, 50] == b) | (meta_s[0, 51] == b)

    def choose(t):
        margin(t, 0).wait_recv()
        own_half(t).wait()

        def body(i, carry):
            at = HALF * slot(b) + i
            lbufs[t][at] = jnp.where(wanted, lbufs[t][at], recv1[t, i])
            return carry

        lax.fori_loop(0, HALF, body, 0)
        for kind in (1, 2, 3):
            margin(t, kind).start()

    def cross(t):
        margin(t, 1).wait_recv()
        for kind in (4, 5):
            margin(t, kind).start()

    def forward(t):
        for kind in (2, 3, 4, 5):
            margin(t, kind).wait_recv()
            margin(t, kind + 4).start()

    def finish(t):
        for kind in (6, 7, 8, 9):
            margin(t, kind).wait_recv()

    step_of = (0, 1 + 2 * core, 2, 3 - 2 * core)

    def spread_margin(t):
        for j in range(STEPS):
            root = meta_s[0, 48 + step_of[j]]

            def body(i, carry):
                r, k = i // KB, lax.rem(i, KB)
                at = group_s[root, 0, i]
                block = lbufs[t][NS * lax.rem(root, 4) + jnp.minimum(at, NS - 1)]
                high, low = split(jnp.where(at < NS, block, 0.0))
                cols = pl.ds(pl.multiple_of(k * bs, bs), bs)
                l_dense[j, pl.ds(pl.multiple_of(r * tr, tr), tr), cols] = high
                l_dense[j, pl.ds(pl.multiple_of((RB + r) * tr, tr), tr), cols] = low
                return carry

            lax.fori_loop(0, RB * KB, body, 0)

    def multiply(t):
        def column(c, carry):
            total = jnp.zeros((RB * tr, bs), F32)
            for j in range(STEPS):
                first = jnp.dot(l_dense[j], rd_hi[j, c], preferred_element_type=F32)
                second = jnp.dot(l_dense[j, : RB * tr, :], rd_lo[j, c], preferred_element_type=F32)
                total = total + (first[: RB * tr] + (first[RB * tr :] + second))
            for r in range(RB):
                acc[r * CB + c] = total[r * tr : (r + 1) * tr]
            return carry

        lax.fori_loop(0, CB, column, 0)

        def keep(m, carry):
            out_v[m, t * tr : (t + 1) * tr, :] = acc[meta_s[0, 64 + m]]
            return carry

        lax.fori_loop(0, NC, keep, 0)
        out(t).start()

    def out(t):
        at = pl.ds(t * tr, tr)
        return pltpu.make_async_copy(out_v.at[:, at], o_hbm.at[:, at], out_sem.at[t])

    choose(0)
    for i in range(10):
        table(i).wait_recv()
    mine_g.wait()
    mine_d.wait()
    to_s = [
        pltpu.make_async_copy(group_v, group_s, local_sem.at[3]),
        pltpu.make_async_copy(density_v, density_s, local_sem.at[4]),
    ]
    for copy in to_s:
        copy.start()
    choose(1)
    cross(0)
    for copy in to_s:
        copy.wait()
    own_density.wait()
    spread_density(r_own, 0, 0)
    choose(2)
    cross(1)
    forward(0)

    for j in range(NR):
        density(1, j).wait_recv()

        @pl.when(relays)
        def _():
            relay(j).start()

    spread_density(r_a, 1, step_of[1])
    choose(3)
    cross(2)
    forward(1)
    cross(3)
    finish(0)
    for j in range(NR):
        density(0, j).wait_recv()
        density(2, j).start()
    spread_density(r_two, 2, 2)
    forward(2)
    spread_margin(0)
    for j in range(NR):
        density(2, j).wait_recv()
    spread_density(r_b, 3, step_of[3])
    forward(3)
    multiply(0)
    for t in range(1, NT):
        finish(t)
        spread_margin(t)
        multiply(t)

    for t in range(NT):
        out(t).wait()
        for kind in range(10):
            margin(t, kind).wait_send()
    for j in range(NR):
        density(1, j).wait_send()
        density(2, j).wait_send()

    @pl.when(direct)
    def _():
        for j in range(NR):
            density(0, j).wait_send()

    @pl.when(relays)
    def _():
        for j in range(NR):
            relay(j).wait_send()

    for i in range(10):
        table(i).wait_send()


def tables(s_list, x_list, c_list, owner):
    def inverse(places, columns, cells, empty):
        cell = places[:, 0] * columns + places[:, 1]
        match = cell[:, None] == jnp.arange(cells)[None, :]
        return jnp.min(jnp.where(match, jnp.arange(places.shape[0])[:, None], empty), axis=0)

    def padded(row, size):
        return jnp.pad(row, (0, size - row.shape[0]))

    row = jnp.concatenate([
        padded(inverse(s_list, KB, RB * KB, NS), 16),
        padded(inverse(x_list, CB, KB * CB, NX), 32),
        padded(owner, 16),
        padded(c_list[:, 0] * CB + c_list[:, 1], 64),
    ])
    return jnp.broadcast_to(row.astype(jnp.int32)[None], (8, 128))


def per_device(s_blocks, s_list, x_blocks, x_list, c_list, owner):
    bs = s_blocks.shape[-1]
    tr = bs // NT
    meta = tables(s_list[0, 0, 0], x_list[0, 0], c_list[0, 0], owner[0])
    any_spec = pl.BlockSpec(memory_space=pl.ANY)
    hbm = pl.BlockSpec(memory_space=pltpu.HBM)
    product = pl.pallas_call(
        kernel,
        out_shape=jax.ShapeDtypeStruct((NC, bs, bs), F32),
        in_specs=[pl.BlockSpec(memory_space=pltpu.SMEM), pl.BlockSpec(memory_space=pltpu.VMEM), hbm, hbm],
        out_specs=hbm,
        scratch_shapes=[pltpu.VMEM((4 * NS, tr, bs), F32)] * NT + [
            pltpu.VMEM((NT, HALF, tr, bs), F32),
            pltpu.VMEM((NX, bs, bs), F32),
            pltpu.VMEM((NX, bs, bs), F32),
            pltpu.VMEM((NX, bs, bs), F32),
            pltpu.VMEM((NX, bs, bs), F32),
            pltpu.VMEM((STEPS, CB, KB * bs, bs), BF16),
            pltpu.VMEM((STEPS, CB, KB * bs, bs), BF16),
            pltpu.VMEM((STEPS, 2 * RB * tr, KB * bs), BF16),
            pltpu.VMEM((RB * CB, tr, bs), F32),
            pltpu.VMEM((NC, bs, bs), F32),
            pltpu.VMEM((8, 8, 128), jnp.int32),
            pltpu.VMEM((4, 8, 128), jnp.int32),
            pltpu.SMEM((8, 8, 128), jnp.int32),
            pltpu.SMEM((4, 8, 128), jnp.int32),
            pltpu.SemaphoreType.DMA((NT, 10)),
            pltpu.SemaphoreType.DMA((NT, 10)),
            pltpu.SemaphoreType.DMA((4, NR)),
            pltpu.SemaphoreType.DMA((3, NR)),
            pltpu.SemaphoreType.DMA((10,)),
            pltpu.SemaphoreType.DMA((10,)),
            pltpu.SemaphoreType.DMA((NT,)),
            pltpu.SemaphoreType.DMA((5,)),
            pltpu.SemaphoreType.DMA((NT,)),
        ],
        compiler_params=pltpu.CompilerParams(
            collective_id=0, has_side_effects=True, vmem_limit_bytes=60 * 1024 * 1024
        ),
        cost_estimate=pl.CostEstimate(flops=20 * 10**9, bytes_accessed=10**7, transcendentals=0),
    )(meta, meta, s_blocks[0, 0, 0], x_blocks[0, 0])
    return product[None, None]


def solution(mesh):
    return jax.shard_map(
        per_device,
        mesh=mesh,
        in_specs=(
            P("loop", "bcast", None, None, None, None),
            P("loop", "bcast", None, None, None),
            P("loop", "bcast", None, None, None),
            P("loop", "bcast", None, None),
            P("loop", "bcast", None, None),
            P("loop", None),
        ),
        out_specs=P("loop", "bcast", None, None, None),
        check_vma=False,
    )
```

```python
import jax
import jax.numpy as jnp
from jax import lax
from jax.experimental import pallas as pl
from jax.experimental.pallas import tpu as pltpu
from jax.sharding import PartitionSpec as P

RB = 3
KB = 4
CB = 4
STEPS = 4
NS = 10
NX = 12
NC = 10
NT = 4
ND = 6
NR = 3
HALF = NS // 2
MESH = pl.DeviceIdType.MESH
BF16 = jnp.bfloat16
F32 = jnp.float32


def kernel(c_s, owner_s, s_places, x_places, s_hbm, x_hbm, o_hbm, *rest):
    lbufs = rest[:NT]
    (recv1, r_own, r_a, r_two, r_b, rd_hi, rd_lo, l_dense, acc, out_v, meta_v, group_v, density_v,
     group_s, density_s, ss, rs, rss, rrs, dss, drs, pss, prs, ms, mr, own_sem, local_sem, out_sem) = rest[NT:]
    bs = s_hbm.shape[-1]
    tr = bs // NT
    n_loop, n_bcast = lax.axis_size("loop"), lax.axis_size("bcast")
    l, b = lax.axis_index("loop"), lax.axis_index("bcast")
    core = lax.rem(l, 2)
    hi_x = lax.rem(l // 2, 2)
    half = b // 4

    def loop_at(by):
        return (lax.rem(l + by + n_loop, n_loop), b)

    def bcast_at(by):
        return (l, lax.rem(b + by + n_bcast, n_bcast))

    def crossed(dev):
        return dev + 1 - 2 * lax.rem(dev, 2)

    def slot(dev):
        return 2 * lax.rem(dev, 4) + dev // 4

    across = (l, crossed(b))
    up, down = bcast_at(2), bcast_at(-2)
    sibling = (l + 1 - 2 * core, b)

    def stands(places, columns, count):
        cell = places[0:1, :] * columns + places[1:2, :]
        position = lax.broadcasted_iota(jnp.int32, (KB * CB, count), 0)
        entry = lax.broadcasted_iota(jnp.int32, (KB * CB, count), 1)
        return jnp.min(jnp.where(cell == position, entry, count), axis=1, keepdims=True)

    lane = lax.broadcasted_iota(jnp.int32, (KB * CB, 128), 1)
    meta_v[...] = jnp.where(lane == 0, stands(s_places, KB, NS), stands(x_places, CB, NX))

    barrier = pltpu.get_barrier_semaphore()
    peers = [bcast_at(i) for i in range(1, 8)] + [loop_at(i) for i in (-3, -2, -1, 1, 2, 3)]
    for peer in peers:
        pl.semaphore_signal(barrier, inc=1, device_id=peer, device_id_type=MESH)
    pl.semaphore_wait(barrier, len(peers))

    def remote(src, dst, send_sem, recv_sem, dev):
        return pltpu.make_async_remote_copy(
            src_ref=src, dst_ref=dst, send_sem=send_sem, recv_sem=recv_sem, device_id=dev, device_id_type=MESH
        )

    def whole(t, dev):
        return lbufs[t].at[pl.ds(HALF * slot(dev), HALF)]

    def part(t, dev, j):
        return lbufs[t].at[pl.ds(HALF * slot(dev), HALF), pl.ds(j * (tr // 2), tr // 2)]

    left, right = down[1], up[1]

    def margin(t, kind):
        if kind == 0:
            src = s_hbm.at[pl.ds(HALF * (1 - half), HALF), pl.ds(t * tr, tr)]
            return remote(src, recv1.at[t], ss.at[t, 0], rs.at[t, 0], bcast_at(4))
        ref, dev = {
            1: (lambda: whole(t, b), across),
            2: (lambda: whole(t, b), up),
            3: (lambda: whole(t, b), down),
            4: (lambda: whole(t, across[1]), up),
            5: (lambda: whole(t, across[1]), down),
            6: (lambda: part(t, left, 0), up),
            7: (lambda: part(t, right, 1), down),
            8: (lambda: part(t, crossed(left), 0), up),
            9: (lambda: part(t, crossed(right), 1), down),
        }[kind]
        return remote(ref(), ref(), ss.at[t, kind], rs.at[t, kind], dev)

    xn = NX // NR

    lower = (lax.rem(l - 3 + 2 * core + n_loop, n_loop), b)

    def density(kind):
        dev, src, dst = {
            1: (lower, x_hbm, r_a),
            2: (sibling, r_two, r_b),
        }[kind]
        return remote(src, dst, rss.at[kind], rrs.at[kind], dev)

    def direct(k):
        at = pl.ds(k * (NX // ND), NX // ND)
        return remote(x_hbm.at[at], r_two.at[at], dss.at[k], drs.at[k], loop_at(-2))

    def relayed(j):
        at = pl.ds(j * xn, xn)
        return remote(x_hbm.at[at], r_a.at[at], pss.at[0, j], prs.at[0, j], lower)

    def relay(j):
        at = pl.ds(j * xn, xn)
        return remote(r_a.at[at], r_two.at[at], pss.at[1, j], prs.at[1, j], loop_at(1))

    gives = jnp.logical_and(hi_x == 0, core == 0)
    relays = jnp.logical_and(hi_x == 0, core == 1)
    takes = jnp.logical_and(hi_x == 1, core == 0)

    def either(flag, then, otherwise):
        pl.when(flag)(then)
        pl.when(jnp.logical_not(flag))(otherwise)

    def own_half(t):
        src = s_hbm.at[pl.ds(HALF * half, HALF), pl.ds(t * tr, tr)]
        return pltpu.make_async_copy(src, whole(t, b), own_sem.at[t])

    def begin(t):
        margin(t, 0).start()
        own_half(t).start()

    def table(i):
        if i < 7:
            return remote(meta_v, group_v.at[b], ms.at[i], mr.at[i], bcast_at(i + 1))
        by = i - 6
        return remote(meta_v, density_v.at[by], ms.at[i], mr.at[i], loop_at(-by))

    for i in range(10):
        table(i).start()
    mine_g = pltpu.make_async_copy(meta_v, group_v.at[b], local_sem.at[1])
    mine_d = pltpu.make_async_copy(meta_v, density_v.at[0], local_sem.at[2])
    mine_g.start()
    mine_d.start()

    begin(0)
    either(gives, lambda: relayed(0).start(), lambda: density(1).start())

    @pl.when(jnp.logical_not(gives))
    def _():
        direct(0).start()
        direct(1).start()

    begin(1)
    own_density = pltpu.make_async_copy(x_hbm, r_own, local_sem.at[0])
    own_density.start()

    def split(block):
        high = block.astype(BF16)
        return high, (block - high.astype(F32)).astype(BF16)

    def spread_density(ref, j, step):
        def body(i, carry):
            k, c = i // CB, lax.rem(i, CB)
            at = density_s[step, i, 1]
            block = jnp.where(at < NX, ref[jnp.minimum(at, NX - 1)], 0.0)
            rows = pl.ds(pl.multiple_of(k * bs, bs), bs)
            high, low = split(block)
            rd_hi[j, c, rows, :] = high
            rd_lo[j, c, rows, :] = low
            return carry

        lax.fori_loop(0, KB * CB, body, 0)

    wanted = (owner_s[0, 0] == b) | (owner_s[0, 1] == b) | (owner_s[0, 2] == b) | (owner_s[0, 3] == b)

    def choose(t):
        margin(t, 0).wait_recv()
        own_half(t).wait()

        def body(i, carry):
            at = HALF * slot(b) + i
            lbufs[t][at] = jnp.where(wanted, lbufs[t][at], recv1[t, i])
            return carry

        lax.fori_loop(0, HALF, body, 0)
        for kind in (1, 2, 3):
            margin(t, kind).start()

    def cross(t):
        margin(t, 1).wait_recv()
        for kind in (4, 5):
            margin(t, kind).start()

    def forward_own(t):
        for kind in (2, 3):
            margin(t, kind).wait_recv()
            margin(t, kind + 4).start()

    def forward_crossed(t):
        for kind in (4, 5):
            margin(t, kind).wait_recv()
            margin(t, kind + 4).start()

    def finish(t):
        for kind in (6, 7, 8, 9):
            margin(t, kind).wait_recv()

    def advance(k):
        @pl.when(jnp.logical_not(gives))
        def _():
            direct(k).wait_send()
            direct(k + 2).start()

    def density_turn(j):
        if j + 1 < NR:

            @pl.when(gives)
            def _():
                relayed(j).wait_send()
                relayed(j + 1).start()

        @pl.when(relays)
        def _():
            relayed(j).wait_recv()
            relay(j).start()

    step_of = (0, 1 + 2 * core, 2, 3 - 2 * core)

    def spread_margin(t):
        for j in range(STEPS):
            root = owner_s[0, step_of[j]]

            def body(i, carry):
                r, k = i // KB, lax.rem(i, KB)
                at = group_s[root, i, 0]
                block = lbufs[t][NS * lax.rem(root, 4) + jnp.minimum(at, NS - 1)]
                high, low = split(jnp.where(at < NS, block, 0.0))
                cols = pl.ds(pl.multiple_of(k * bs, bs), bs)
                l_dense[t % 2, j, pl.ds(pl.multiple_of(r * tr, tr), tr), cols] = high
                l_dense[t % 2, j, pl.ds(pl.multiple_of((RB + r) * tr, tr), tr), cols] = low
                return carry

            lax.fori_loop(0, RB * KB, body, 0)

    def multiply(t, terms):
        def column(c, carry):
            total = jnp.zeros((RB * tr, bs), F32)
            for j in terms:
                first = jnp.dot(l_dense[t % 2, j], rd_hi[j, c], preferred_element_type=F32)
                second = jnp.dot(l_dense[t % 2, j, : RB * tr, :], rd_lo[j, c], preferred_element_type=F32)
                total = total + (first[: RB * tr] + (first[RB * tr :] + second))
            for r in range(RB):
                piece = total[r * tr : (r + 1) * tr]
                acc[t, r * CB + c] = piece if terms[0] == 0 else acc[t, r * CB + c] + piece
            return carry

        lax.fori_loop(0, CB, column, 0)

    def keep(t):
        def body(m, carry):
            out_v[m, t * tr : (t + 1) * tr, :] = acc[t, c_s[0, m] * CB + c_s[1, m]]
            return carry

        lax.fori_loop(0, NC, body, 0)
        out(t).start()

    def out(t):
        at = pl.ds(t * tr, tr)
        return pltpu.make_async_copy(out_v.at[:, at], o_hbm.at[:, at], out_sem.at[t])

    for i in range(10):
        table(i).wait_recv()
    mine_g.wait()
    mine_d.wait()
    to_s = [
        pltpu.make_async_copy(group_v, group_s, local_sem.at[3]),
        pltpu.make_async_copy(density_v, density_s, local_sem.at[4]),
    ]
    for copy in to_s:
        copy.start()
    choose(0)
    begin(2)
    advance(0)
    choose(1)
    begin(3)
    for copy in to_s:
        copy.wait()
    cross(0)
    density_turn(0)
    advance(1)
    forward_own(0)
    choose(2)
    cross(1)
    own_density.wait()
    spread_density(r_own, 0, 0)
    advance(2)
    forward_crossed(0)
    density_turn(1)
    forward_own(1)
    choose(3)
    cross(2)
    advance(3)
    forward_crossed(1)
    density_turn(2)
    forward_own(2)
    finish(0)
    cross(3)
    pl.when(jnp.logical_not(relays))(lambda: density(1).wait_recv())
    spread_density(r_a, 1, step_of[1])
    forward_crossed(2)
    forward_own(3)
    spread_margin(0)
    multiply(0, (0, 1))
    finish(1)
    forward_crossed(3)
    spread_margin(1)
    multiply(1, (0, 1))

    def parts_in():
        for j in range(NR):
            relay(j).wait_recv()

    def direct_in():
        for k in range(ND):
            direct(k).wait_recv()

    either(takes, parts_in, direct_in)
    density(2).start()
    spread_density(r_two, 2, 2)
    density(2).wait_recv()
    spread_density(r_b, 3, step_of[3])
    multiply(0, (2, 3))
    keep(0)
    multiply(1, (2, 3))
    keep(1)
    for t in range(2, NT):
        finish(t)
        spread_margin(t)
        multiply(t, (0, 1, 2, 3))
        keep(t)

    for t in range(NT):
        out(t).wait()
        for kind in range(10):
            margin(t, kind).wait_send()
    density(2).wait_send()

    def sent():
        density(1).wait_send()
        for k in range(ND - 2, ND):
            direct(k).wait_send()

    either(gives, lambda: relayed(NR - 1).wait_send(), sent)

    @pl.when(relays)
    def _():
        for j in range(NR):
            relay(j).wait_send()

    for i in range(10):
        table(i).wait_send()


def per_device(s_blocks, s_list, x_blocks, x_list, c_list, owner):
    bs = s_blocks.shape[-1]
    tr = bs // NT
    smem = pl.BlockSpec(memory_space=pltpu.SMEM)
    vmem = pl.BlockSpec(memory_space=pltpu.VMEM)
    hbm = pl.BlockSpec(memory_space=pltpu.HBM)
    product = pl.pallas_call(
        kernel,
        out_shape=jax.ShapeDtypeStruct((NC, bs, bs), F32),
        in_specs=[smem, smem, vmem, vmem, hbm, hbm],
        out_specs=hbm,
        scratch_shapes=[pltpu.VMEM((4 * NS, tr, bs), F32)] * NT + [
            pltpu.VMEM((NT, HALF, tr, bs), F32),
            pltpu.VMEM((NX, bs, bs), F32),
            pltpu.VMEM((NX, bs, bs), F32),
            pltpu.VMEM((NX, bs, bs), F32),
            pltpu.VMEM((NX, bs, bs), F32),
            pltpu.VMEM((STEPS, CB, KB * bs, bs), BF16),
            pltpu.VMEM((STEPS, CB, KB * bs, bs), BF16),
            pltpu.VMEM((2, STEPS, 2 * RB * tr, KB * bs), BF16),
            pltpu.VMEM((NT, RB * CB, tr, bs), F32),
            pltpu.VMEM((NC, bs, bs), F32),
            pltpu.VMEM((KB * CB, 128), jnp.int32),
            pltpu.VMEM((8, KB * CB, 128), jnp.int32),
            pltpu.VMEM((4, KB * CB, 128), jnp.int32),
            pltpu.SMEM((8, KB * CB, 128), jnp.int32),
            pltpu.SMEM((4, KB * CB, 128), jnp.int32),
            pltpu.SemaphoreType.DMA((NT, 10)),
            pltpu.SemaphoreType.DMA((NT, 10)),
            pltpu.SemaphoreType.DMA((3,)),
            pltpu.SemaphoreType.DMA((3,)),
            pltpu.SemaphoreType.DMA((ND,)),
            pltpu.SemaphoreType.DMA((ND,)),
            pltpu.SemaphoreType.DMA((2, NR)),
            pltpu.SemaphoreType.DMA((2, NR)),
            pltpu.SemaphoreType.DMA((10,)),
            pltpu.SemaphoreType.DMA((10,)),
            pltpu.SemaphoreType.DMA((NT,)),
            pltpu.SemaphoreType.DMA((5,)),
            pltpu.SemaphoreType.DMA((NT,)),
        ],
        compiler_params=pltpu.CompilerParams(
            collective_id=0, has_side_effects=True, vmem_limit_bytes=60 * 1024 * 1024
        ),
        cost_estimate=pl.CostEstimate(flops=20 * 10**9, bytes_accessed=10**7, transcendentals=0),
    )(c_list[0, 0].T, owner, s_list[0, 0, 0].T, x_list[0, 0].T, s_blocks[0, 0, 0], x_blocks[0, 0])
    return product[None, None]


def solution(mesh):
    return jax.shard_map(
        per_device,
        mesh=mesh,
        in_specs=(
            P("loop", "bcast", None, None, None, None),
            P("loop", "bcast", None, None, None),
            P("loop", "bcast", None, None, None),
            P("loop", "bcast", None, None),
            P("loop", "bcast", None, None),
            P("loop", None),
        ),
        out_specs=P("loop", "bcast", None, None, None),
        check_vma=False,
    )
```

```python
import jax
import jax.numpy as jnp
from jax import lax
from jax.experimental import pallas as pl
from jax.experimental.pallas import tpu as pltpu
from jax.sharding import PartitionSpec as P

RB = 3
KB = 4
CB = 4
STEPS = 4
NS = 10
NX = 12
NC = 10
ROWS = (64, 80, 64, 48)
NT = len(ROWS)
STARTS = tuple(sum(ROWS[:t]) for t in range(NT))
ND = 6
NR = 3
HALF = NS // 2
MESH = pl.DeviceIdType.MESH
BF16 = jnp.bfloat16
F32 = jnp.float32


def kernel(c_s, owner_s, s_places, x_places, s_hbm, x_hbm, o_hbm, *rest):
    lbufs, accs = rest[:NT], rest[NT : 2 * NT]
    (recv1, r_own, r_a, r_two, r_b, rd_hi, rd_lo, l_dense, out_v, meta_v, group_v, density_v,
     group_s, density_s, ss, rs, rss, rrs, dss, drs, pss, prs, ms, mr, own_sem, local_sem, out_sem) = rest[2 * NT :]
    bs = s_hbm.shape[-1]
    n_loop, n_bcast = lax.axis_size("loop"), lax.axis_size("bcast")
    l, b = lax.axis_index("loop"), lax.axis_index("bcast")
    core = lax.rem(l, 2)
    hi_x = lax.rem(l // 2, 2)
    half = b // 4

    def loop_at(by):
        return (lax.rem(l + by + n_loop, n_loop), b)

    def bcast_at(by):
        return (l, lax.rem(b + by + n_bcast, n_bcast))

    def crossed(dev):
        return dev + 1 - 2 * lax.rem(dev, 2)

    def slot(dev):
        return 2 * lax.rem(dev, 4) + dev // 4

    across = (l, crossed(b))
    up, down = bcast_at(2), bcast_at(-2)
    sibling = (l + 1 - 2 * core, b)

    def stands(places, columns, count):
        cell = places[0:1, :] * columns + places[1:2, :]
        position = lax.broadcasted_iota(jnp.int32, (KB * CB, count), 0)
        entry = lax.broadcasted_iota(jnp.int32, (KB * CB, count), 1)
        return jnp.min(jnp.where(cell == position, entry, count), axis=1, keepdims=True)

    lane = lax.broadcasted_iota(jnp.int32, (KB * CB, 128), 1)
    meta_v[...] = jnp.where(lane == 0, stands(s_places, KB, NS), stands(x_places, CB, NX))

    barrier = pltpu.get_barrier_semaphore()
    peers = [bcast_at(i) for i in range(1, 8)] + [loop_at(i) for i in (-3, -2, -1, 1, 2, 3)]
    for peer in peers:
        pl.semaphore_signal(barrier, inc=1, device_id=peer, device_id_type=MESH)
    pl.semaphore_wait(barrier, len(peers))

    def remote(src, dst, send_sem, recv_sem, dev):
        return pltpu.make_async_remote_copy(
            src_ref=src, dst_ref=dst, send_sem=send_sem, recv_sem=recv_sem, device_id=dev, device_id_type=MESH
        )

    def whole(t, dev):
        return lbufs[t].at[pl.ds(HALF * slot(dev), HALF)]

    def part(t, dev, j):
        return lbufs[t].at[pl.ds(HALF * slot(dev), HALF), pl.ds(j * (ROWS[t] // 2), ROWS[t] // 2)]

    left, right = down[1], up[1]

    def margin(t, kind):
        if kind == 0:
            rows = pl.ds(STARTS[t], ROWS[t])
            src = s_hbm.at[pl.ds(HALF * (1 - half), HALF), rows]
            return remote(src, recv1.at[:, rows], ss.at[t, 0], rs.at[t, 0], bcast_at(4))
        ref, dev = {
            1: (lambda: whole(t, b), across),
            2: (lambda: whole(t, b), up),
            3: (lambda: whole(t, b), down),
            4: (lambda: whole(t, across[1]), up),
            5: (lambda: whole(t, across[1]), down),
            6: (lambda: part(t, left, 0), up),
            7: (lambda: part(t, right, 1), down),
            8: (lambda: part(t, crossed(left), 0), up),
            9: (lambda: part(t, crossed(right), 1), down),
        }[kind]
        return remote(ref(), ref(), ss.at[t, kind], rs.at[t, kind], dev)

    xn = NX // NR

    lower = (lax.rem(l - 3 + 2 * core + n_loop, n_loop), b)

    def density(kind):
        dev, src, dst = {
            1: (lower, x_hbm, r_a),
        }[kind]
        return remote(src, dst, rss.at[kind], rrs.at[kind], dev)

    def shared(j):
        at = pl.ds(j * xn, xn)
        return remote(r_two.at[at], r_b.at[at], pss.at[2, j], prs.at[2, j], sibling)

    def direct(k):
        at = pl.ds(k * (NX // ND), NX // ND)
        return remote(x_hbm.at[at], r_two.at[at], dss.at[k], drs.at[k], loop_at(-2))

    def relayed(j):
        at = pl.ds(j * xn, xn)
        return remote(x_hbm.at[at], r_a.at[at], pss.at[0, j], prs.at[0, j], lower)

    def relay(j):
        at = pl.ds(j * xn, xn)
        return remote(r_a.at[at], r_two.at[at], pss.at[1, j], prs.at[1, j], loop_at(1))

    gives = jnp.logical_and(hi_x == 0, core == 0)
    relays = jnp.logical_and(hi_x == 0, core == 1)
    takes = jnp.logical_and(hi_x == 1, core == 0)

    def either(flag, then, otherwise):
        pl.when(flag)(then)
        pl.when(jnp.logical_not(flag))(otherwise)

    def own_half(t):
        src = s_hbm.at[pl.ds(HALF * half, HALF), pl.ds(STARTS[t], ROWS[t])]
        return pltpu.make_async_copy(src, whole(t, b), own_sem.at[t])

    def begin(t):
        margin(t, 0).start()
        own_half(t).start()

    def table(i):
        if i < 7:
            return remote(meta_v, group_v.at[b], ms.at[i], mr.at[i], bcast_at(i + 1))
        by = i - 6
        return remote(meta_v, density_v.at[by], ms.at[i], mr.at[i], loop_at(-by))

    for i in range(10):
        table(i).start()
    mine_g = pltpu.make_async_copy(meta_v, group_v.at[b], local_sem.at[1])
    mine_d = pltpu.make_async_copy(meta_v, density_v.at[0], local_sem.at[2])
    mine_g.start()
    mine_d.start()

    begin(0)
    either(gives, lambda: relayed(0).start(), lambda: density(1).start())

    @pl.when(jnp.logical_not(gives))
    def _():
        direct(0).start()
        direct(1).start()

    begin(1)
    own_density = pltpu.make_async_copy(x_hbm, r_own, local_sem.at[0])
    own_density.start()

    def split(block):
        high = block.astype(BF16)
        return high, (block - high.astype(F32)).astype(BF16)

    def spread_density(ref, j, step):
        def body(i, carry):
            k, c = i // CB, lax.rem(i, CB)
            at = density_s[step, i, 1]
            block = jnp.where(at < NX, ref[jnp.minimum(at, NX - 1)], 0.0)
            rows = pl.ds(pl.multiple_of(k * bs, bs), bs)
            high, low = split(block)
            rd_hi[j, c, rows, :] = high
            rd_lo[j, c, rows, :] = low
            return carry

        lax.fori_loop(0, KB * CB, body, 0)

    wanted = (owner_s[0, 0] == b) | (owner_s[0, 1] == b) | (owner_s[0, 2] == b) | (owner_s[0, 3] == b)

    def choose(t):
        margin(t, 0).wait_recv()
        own_half(t).wait()

        def body(i, carry):
            at = HALF * slot(b) + i
            lbufs[t][at] = jnp.where(wanted, lbufs[t][at], recv1[i, STARTS[t] : STARTS[t] + ROWS[t], :])
            return carry

        lax.fori_loop(0, HALF, body, 0)
        for kind in (1, 2, 3):
            margin(t, kind).start()

    def cross(t):
        margin(t, 1).wait_recv()
        for kind in (4, 5):
            margin(t, kind).start()

    def forward_own(t):
        for kind in (2, 3):
            margin(t, kind).wait_recv()
            margin(t, kind + 4).start()

    def forward_crossed(t):
        for kind in (4, 5):
            margin(t, kind).wait_recv()
            margin(t, kind + 4).start()

    def finish(t):
        for kind in (6, 7, 8, 9):
            margin(t, kind).wait_recv()

    def advance(k):
        @pl.when(jnp.logical_not(gives))
        def _():
            direct(k).wait_send()
            direct(k + 2).start()

    def share(j):
        each = ND // NR

        def direct_in():
            for k in range(each * j, each * (j + 1)):
                direct(k).wait_recv()

        either(takes, lambda: relay(j).wait_recv(), direct_in)
        shared(j).start()

    def density_turn(j):
        if j + 1 < NR:

            @pl.when(gives)
            def _():
                relayed(j).wait_send()
                relayed(j + 1).start()

        @pl.when(relays)
        def _():
            relayed(j).wait_recv()
            relay(j).start()

    step_of = (0, 1 + 2 * core, 2, 3 - 2 * core)

    def spread_margin(t):
        for j in range(STEPS):
            root, tr = owner_s[0, step_of[j]], ROWS[t]

            def body(i, carry):
                r, k = i // KB, lax.rem(i, KB)
                at = group_s[root, i, 0]
                block = lbufs[t][NS * lax.rem(root, 4) + jnp.minimum(at, NS - 1)]
                high, low = split(jnp.where(at < NS, block, 0.0))
                cols = pl.ds(pl.multiple_of(k * bs, bs), bs)
                l_dense[t % 2, j, pl.ds(pl.multiple_of(r * tr, tr), tr), cols] = high
                l_dense[t % 2, j, pl.ds(pl.multiple_of((RB + r) * tr, tr), tr), cols] = low
                return carry

            lax.fori_loop(0, RB * KB, body, 0, unroll=2)

    def multiply(t, terms):
        tr, acc = ROWS[t], accs[t]

        def column(c, carry):
            total = jnp.zeros((RB * tr, bs), F32)
            for j in terms:
                first = jnp.dot(l_dense[t % 2, j, : 2 * RB * tr, :], rd_hi[j, c], preferred_element_type=F32)
                second = jnp.dot(l_dense[t % 2, j, : RB * tr, :], rd_lo[j, c], preferred_element_type=F32)
                total = total + (first[: RB * tr] + (first[RB * tr :] + second))
            for r in range(RB):
                piece = total[r * tr : (r + 1) * tr]
                acc[r * CB + c] = piece if terms[0] == 0 else acc[r * CB + c] + piece
            return carry

        lax.fori_loop(0, CB, column, 0)

    def keep(t):
        def body(m, carry):
            out_v[m, STARTS[t] : STARTS[t] + ROWS[t], :] = accs[t][c_s[0, m] * CB + c_s[1, m]]
            return carry

        lax.fori_loop(0, NC, body, 0)
        out(t).start()

    def out(t):
        at = pl.ds(STARTS[t], ROWS[t])
        return pltpu.make_async_copy(out_v.at[:, at], o_hbm.at[:, at], out_sem.at[t])

    for i in range(10):
        table(i).wait_recv()
    mine_g.wait()
    mine_d.wait()
    to_s = [
        pltpu.make_async_copy(group_v, group_s, local_sem.at[3]),
        pltpu.make_async_copy(density_v, density_s, local_sem.at[4]),
    ]
    for copy in to_s:
        copy.start()
    choose(0)
    begin(2)
    advance(0)
    choose(1)
    begin(3)
    for copy in to_s:
        copy.wait()
    cross(0)
    density_turn(0)
    advance(1)
    forward_own(0)
    choose(2)
    cross(1)
    own_density.wait()
    spread_density(r_own, 0, 0)
    advance(2)
    forward_crossed(0)
    density_turn(1)
    forward_own(1)
    choose(3)
    cross(2)
    advance(3)
    forward_crossed(1)
    density_turn(2)
    share(0)
    forward_own(2)
    cross(3)
    finish(0)
    pl.when(jnp.logical_not(relays))(lambda: density(1).wait_recv())
    spread_density(r_a, 1, step_of[1])
    spread_margin(0)
    multiply(0, (0, 1))
    share(1)
    forward_crossed(2)
    forward_own(3)

    share(2)
    spread_density(r_two, 2, 2)
    finish(1)
    spread_margin(1)
    multiply(1, (0, 1))
    for j in range(NR):
        shared(j).wait_recv()
    spread_density(r_b, 3, step_of[3])
    multiply(0, (2, 3))
    keep(0)
    forward_crossed(3)
    multiply(1, (2, 3))
    keep(1)
    for t in range(2, NT):
        finish(t)
        spread_margin(t)
        multiply(t, (0, 1, 2, 3))
        keep(t)

    for t in range(NT):
        out(t).wait()
        for kind in range(10):
            margin(t, kind).wait_send()
    for j in range(NR):
        shared(j).wait_send()

    def sent():
        density(1).wait_send()
        for k in range(ND - 2, ND):
            direct(k).wait_send()

    either(gives, lambda: relayed(NR - 1).wait_send(), sent)

    @pl.when(relays)
    def _():
        for j in range(NR):
            relay(j).wait_send()

    for i in range(10):
        table(i).wait_send()


def per_device(s_blocks, s_list, x_blocks, x_list, c_list, owner):
    bs = s_blocks.shape[-1]
    smem = pl.BlockSpec(memory_space=pltpu.SMEM)
    vmem = pl.BlockSpec(memory_space=pltpu.VMEM)
    hbm = pl.BlockSpec(memory_space=pltpu.HBM)
    product = pl.pallas_call(
        kernel,
        out_shape=jax.ShapeDtypeStruct((NC, bs, bs), F32),
        in_specs=[smem, smem, vmem, vmem, hbm, hbm],
        out_specs=hbm,
        scratch_shapes=[
            *(pltpu.VMEM((4 * NS, tr, bs), F32) for tr in ROWS),
            *(pltpu.VMEM((RB * CB, tr, bs), F32) for tr in ROWS),
            pltpu.VMEM((HALF, bs, bs), F32),
            pltpu.VMEM((NX, bs, bs), F32),
            pltpu.VMEM((NX, bs, bs), F32),
            pltpu.VMEM((NX, bs, bs), F32),
            pltpu.VMEM((NX, bs, bs), F32),
            pltpu.VMEM((STEPS, CB, KB * bs, bs), BF16),
            pltpu.VMEM((STEPS, CB, KB * bs, bs), BF16),
            pltpu.VMEM((2, STEPS, 2 * RB * max(ROWS), KB * bs), BF16),
            pltpu.VMEM((NC, bs, bs), F32),
            pltpu.VMEM((KB * CB, 128), jnp.int32),
            pltpu.VMEM((8, KB * CB, 128), jnp.int32),
            pltpu.VMEM((4, KB * CB, 128), jnp.int32),
            pltpu.SMEM((8, KB * CB, 128), jnp.int32),
            pltpu.SMEM((4, KB * CB, 128), jnp.int32),
            pltpu.SemaphoreType.DMA((NT, 10)),
            pltpu.SemaphoreType.DMA((NT, 10)),
            pltpu.SemaphoreType.DMA((2,)),
            pltpu.SemaphoreType.DMA((2,)),
            pltpu.SemaphoreType.DMA((ND,)),
            pltpu.SemaphoreType.DMA((ND,)),
            pltpu.SemaphoreType.DMA((3, NR)),
            pltpu.SemaphoreType.DMA((3, NR)),
            pltpu.SemaphoreType.DMA((10,)),
            pltpu.SemaphoreType.DMA((10,)),
            pltpu.SemaphoreType.DMA((NT,)),
            pltpu.SemaphoreType.DMA((5,)),
            pltpu.SemaphoreType.DMA((NT,)),
        ],
        compiler_params=pltpu.CompilerParams(
            collective_id=0, has_side_effects=True, vmem_limit_bytes=60 * 1024 * 1024
        ),
        cost_estimate=pl.CostEstimate(flops=20 * 10**9, bytes_accessed=10**7, transcendentals=0),
    )(c_list[0, 0].T, owner, s_list[0, 0, 0].T, x_list[0, 0].T, s_blocks[0, 0, 0], x_blocks[0, 0])
    return product[None, None]


def solution(mesh):
    return jax.shard_map(
        per_device,
        mesh=mesh,
        in_specs=(
            P("loop", "bcast", None, None, None, None),
            P("loop", "bcast", None, None, None),
            P("loop", "bcast", None, None, None),
            P("loop", "bcast", None, None),
            P("loop", "bcast", None, None),
            P("loop", None),
        ),
        out_specs=P("loop", "bcast", None, None, None),
        check_vma=False,
    )
```

```python
import jax
import jax.numpy as jnp
from jax import lax
from jax.experimental import pallas as pl
from jax.experimental.pallas import tpu as pltpu
from jax.sharding import PartitionSpec as P

RB = 3
KB = 4
CB = 4
STEPS = 4
NS = 10
NX = 12
NC = 10
ROWS = (64, 80, 64, 48)
NT = len(ROWS)
STARTS = tuple(sum(ROWS[:t]) for t in range(NT))
ND = 6
NR = 3
HALF = NS // 2
MESH = pl.DeviceIdType.MESH
BF16 = jnp.bfloat16
F32 = jnp.float32


def kernel(c_s, owner_s, s_places, x_places, s_hbm, x_hbm, o_hbm, *rest):
    lbufs, accs = rest[:NT], rest[NT : 2 * NT]
    (recv1, r_own, r_a, r_two, r_b, rd_hi, rd_lo, l_dense, out_v, meta_v, group_v, density_v,
     group_s, density_s, ss, rs, rss, rrs, dss, drs, pss, prs, ms, mr, own_sem, local_sem, out_sem) = rest[2 * NT :]
    bs = s_hbm.shape[-1]
    n_loop, n_bcast = lax.axis_size("loop"), lax.axis_size("bcast")
    l, b = lax.axis_index("loop"), lax.axis_index("bcast")
    core = lax.rem(l, 2)
    hi_x = lax.rem(l // 2, 2)
    half = b // 4

    def loop_at(by):
        return (lax.rem(l + by + n_loop, n_loop), b)

    def bcast_at(by):
        return (l, lax.rem(b + by + n_bcast, n_bcast))

    def crossed(dev):
        return dev + 1 - 2 * lax.rem(dev, 2)

    def slot(dev):
        return 2 * lax.rem(dev, 4) + dev // 4

    across = (l, crossed(b))
    up, down = bcast_at(2), bcast_at(-2)
    sibling = (l + 1 - 2 * core, b)

    def stands(places, columns, count):
        cell = places[0:1, :] * columns + places[1:2, :]
        position = lax.broadcasted_iota(jnp.int32, (KB * CB, count), 0)
        entry = lax.broadcasted_iota(jnp.int32, (KB * CB, count), 1)
        return jnp.min(jnp.where(cell == position, entry, count), axis=1, keepdims=True)

    lane = lax.broadcasted_iota(jnp.int32, (KB * CB, 128), 1)
    meta_v[...] = jnp.where(lane == 0, stands(s_places, KB, NS), stands(x_places, CB, NX))

    barrier = pltpu.get_barrier_semaphore()
    peers = [bcast_at(i) for i in range(1, 8)] + [loop_at(i) for i in (-3, -2, -1, 1, 2, 3)]
    for peer in peers:
        pl.semaphore_signal(barrier, inc=1, device_id=peer, device_id_type=MESH)
    pl.semaphore_wait(barrier, len(peers))

    def remote(src, dst, send_sem, recv_sem, dev):
        return pltpu.make_async_remote_copy(
            src_ref=src, dst_ref=dst, send_sem=send_sem, recv_sem=recv_sem, device_id=dev, device_id_type=MESH
        )

    def whole(t, dev):
        return lbufs[t].at[pl.ds(HALF * slot(dev), HALF)]

    def part(t, dev, j):
        return lbufs[t].at[pl.ds(HALF * slot(dev), HALF), pl.ds(j * (ROWS[t] // 2), ROWS[t] // 2)]

    left, right = down[1], up[1]

    def margin(t, kind):
        if kind == 0:
            rows = pl.ds(STARTS[t], ROWS[t])
            src = s_hbm.at[pl.ds(HALF * (1 - half), HALF), rows]
            return remote(src, recv1.at[:, rows], ss.at[t, 0], rs.at[t, 0], bcast_at(4))
        ref, dev = {
            1: (lambda: whole(t, b), across),
            2: (lambda: whole(t, b), up),
            3: (lambda: whole(t, b), down),
            4: (lambda: whole(t, across[1]), up),
            5: (lambda: whole(t, across[1]), down),
            6: (lambda: part(t, left, 0), up),
            7: (lambda: part(t, right, 1), down),
            8: (lambda: part(t, crossed(left), 0), up),
            9: (lambda: part(t, crossed(right), 1), down),
        }[kind]
        return remote(ref(), ref(), ss.at[t, kind], rs.at[t, kind], dev)

    xn = NX // NR

    lower = (lax.rem(l - 3 + 2 * core + n_loop, n_loop), b)

    def density(kind):
        dev, src, dst = {
            1: (lower, x_hbm, r_a),
        }[kind]
        return remote(src, dst, rss.at[kind], rrs.at[kind], dev)

    def shared(j):
        at = pl.ds(j * xn, xn)
        return remote(r_two.at[at], r_b.at[at], pss.at[2, j], prs.at[2, j], sibling)

    def direct(k):
        at = pl.ds(k * (NX // ND), NX // ND)
        return remote(x_hbm.at[at], r_two.at[at], dss.at[k], drs.at[k], loop_at(-2))

    def relayed(j):
        at = pl.ds(j * xn, xn)
        return remote(x_hbm.at[at], r_a.at[at], pss.at[0, j], prs.at[0, j], lower)

    def relay(j):
        at = pl.ds(j * xn, xn)
        return remote(r_a.at[at], r_two.at[at], pss.at[1, j], prs.at[1, j], loop_at(1))

    gives = jnp.logical_and(hi_x == 0, core == 0)
    relays = jnp.logical_and(hi_x == 0, core == 1)
    takes = jnp.logical_and(hi_x == 1, core == 0)

    def either(flag, then, otherwise):
        pl.when(flag)(then)
        pl.when(jnp.logical_not(flag))(otherwise)

    def own_half(t):
        src = s_hbm.at[pl.ds(HALF * half, HALF), pl.ds(STARTS[t], ROWS[t])]
        return pltpu.make_async_copy(src, whole(t, b), own_sem.at[t])

    def begin(t):
        margin(t, 0).start()
        own_half(t).start()

    def table(i):
        if i < 7:
            return remote(meta_v, group_v.at[b], ms.at[i], mr.at[i], bcast_at(i + 1))
        by = i - 6
        return remote(meta_v, density_v.at[by], ms.at[i], mr.at[i], loop_at(-by))

    begin(0)
    begin(1)
    for i in range(10):
        table(i).start()
    mine_g = pltpu.make_async_copy(meta_v, group_v.at[b], local_sem.at[1])
    mine_d = pltpu.make_async_copy(meta_v, density_v.at[0], local_sem.at[2])
    mine_g.start()
    mine_d.start()

    either(gives, lambda: relayed(0).start(), lambda: density(1).start())

    @pl.when(jnp.logical_not(gives))
    def _():
        direct(0).start()
        direct(1).start()

    own_density = pltpu.make_async_copy(x_hbm, r_own, local_sem.at[0])
    own_density.start()

    def split(block):
        high = block.astype(BF16)
        return high, (block - high.astype(F32)).astype(BF16)

    def spread_density(ref, j, step):
        def body(i, carry):
            k, c = i // CB, lax.rem(i, CB)
            at = density_s[step, i, 1]
            block = jnp.where(at < NX, ref[jnp.minimum(at, NX - 1)], 0.0)
            rows = pl.ds(pl.multiple_of(k * bs, bs), bs)
            high, low = split(block)
            rd_hi[j, c, rows, :] = high
            rd_lo[j, c, rows, :] = low
            return carry

        lax.fori_loop(0, KB * CB, body, 0)

    wanted = (owner_s[0, 0] == b) | (owner_s[0, 1] == b) | (owner_s[0, 2] == b) | (owner_s[0, 3] == b)

    def choose(t):
        margin(t, 0).wait_recv()
        own_half(t).wait()

        def body(i, carry):
            at = HALF * slot(b) + i
            lbufs[t][at] = jnp.where(wanted, lbufs[t][at], recv1[i, STARTS[t] : STARTS[t] + ROWS[t], :])
            return carry

        lax.fori_loop(0, HALF, body, 0)
        for kind in (1, 2, 3):
            margin(t, kind).start()

    def cross(t):
        margin(t, 1).wait_recv()
        for kind in (4, 5):
            margin(t, kind).start()

    def forward_own(t):
        for kind in (2, 3):
            margin(t, kind).wait_recv()
            margin(t, kind + 4).start()

    def forward_crossed(t):
        for kind in (4, 5):
            margin(t, kind).wait_recv()
            margin(t, kind + 4).start()

    def finish(t):
        for kind in (6, 7, 8, 9):
            margin(t, kind).wait_recv()

    def advance(k):
        @pl.when(jnp.logical_not(gives))
        def _():
            direct(k).wait_send()
            direct(k + 2).start()

    def share(j):
        each = ND // NR

        def direct_in():
            for k in range(each * j, each * (j + 1)):
                direct(k).wait_recv()

        either(takes, lambda: relay(j).wait_recv(), direct_in)
        shared(j).start()

    def density_turn(j):
        if j + 1 < NR:

            @pl.when(gives)
            def _():
                relayed(j).wait_send()
                relayed(j + 1).start()

        @pl.when(relays)
        def _():
            relayed(j).wait_recv()
            relay(j).start()

    step_of = (0, 1 + 2 * core, 2, 3 - 2 * core)

    def spread_margin(t):
        for j in range(STEPS):
            root, tr = owner_s[0, step_of[j]], ROWS[t]

            def body(i, carry):
                r, k = i // KB, lax.rem(i, KB)
                at = group_s[root, i, 0]
                block = lbufs[t][NS * lax.rem(root, 4) + jnp.minimum(at, NS - 1)]
                high, low = split(jnp.where(at < NS, block, 0.0))
                cols = pl.ds(pl.multiple_of(k * bs, bs), bs)
                l_dense[t % 2, j, pl.ds(pl.multiple_of(r * tr, tr), tr), cols] = high
                l_dense[t % 2, j, pl.ds(pl.multiple_of((RB + r) * tr, tr), tr), cols] = low
                return carry

            lax.fori_loop(0, RB * KB, body, 0, unroll=4)

    def multiply(t, terms):
        tr, acc = ROWS[t], accs[t]

        def column(c, carry):
            total = jnp.zeros((RB * tr, bs), F32)
            for j in terms:
                first = jnp.dot(l_dense[t % 2, j, : 2 * RB * tr, :], rd_hi[j, c], preferred_element_type=F32)
                second = jnp.dot(l_dense[t % 2, j, : RB * tr, :], rd_lo[j, c], preferred_element_type=F32)
                total = total + (first[: RB * tr] + (first[RB * tr :] + second))
            for r in range(RB):
                piece = total[r * tr : (r + 1) * tr]
                acc[r * CB + c] = piece if terms[0] == 0 else acc[r * CB + c] + piece
            return carry

        lax.fori_loop(0, CB, column, 0)

    def keep(t):
        def body(m, carry):
            out_v[m, STARTS[t] : STARTS[t] + ROWS[t], :] = accs[t][c_s[0, m] * CB + c_s[1, m]]
            return carry

        lax.fori_loop(0, NC, body, 0)
        out(t).start()

    def out(t):
        at = pl.ds(STARTS[t], ROWS[t])
        return pltpu.make_async_copy(out_v.at[:, at], o_hbm.at[:, at], out_sem.at[t])

    choose(0)
    begin(2)
    advance(0)
    choose(1)
    begin(3)
    cross(0)
    for i in range(10):
        table(i).wait_recv()
    mine_g.wait()
    mine_d.wait()
    to_s = [
        pltpu.make_async_copy(group_v, group_s, local_sem.at[3]),
        pltpu.make_async_copy(density_v, density_s, local_sem.at[4]),
    ]
    for copy in to_s:
        copy.start()
    density_turn(0)
    advance(1)
    forward_own(0)
    choose(2)
    cross(1)
    for copy in to_s:
        copy.wait()
    own_density.wait()
    spread_density(r_own, 0, 0)
    advance(2)
    forward_crossed(0)
    density_turn(1)
    forward_own(1)
    choose(3)
    cross(2)
    advance(3)
    forward_crossed(1)
    density_turn(2)
    share(0)
    forward_own(2)
    cross(3)
    finish(0)
    pl.when(jnp.logical_not(relays))(lambda: density(1).wait_recv())
    spread_density(r_a, 1, step_of[1])
    spread_margin(0)
    multiply(0, (0, 1))
    share(1)
    forward_crossed(2)
    forward_own(3)

    share(2)
    spread_density(r_two, 2, 2)
    finish(1)
    spread_margin(1)
    multiply(1, (0, 1))
    for j in range(NR):
        shared(j).wait_recv()
    spread_density(r_b, 3, step_of[3])
    multiply(0, (2, 3))
    keep(0)
    forward_crossed(3)
    multiply(1, (2, 3))
    keep(1)
    for t in range(2, NT):
        finish(t)
        spread_margin(t)
        multiply(t, (0, 1, 2, 3))
        keep(t)

    for t in range(NT):
        out(t).wait()
        for kind in range(10):
            margin(t, kind).wait_send()
    for j in range(NR):
        shared(j).wait_send()

    def sent():
        density(1).wait_send()
        for k in range(ND - 2, ND):
            direct(k).wait_send()

    either(gives, lambda: relayed(NR - 1).wait_send(), sent)

    @pl.when(relays)
    def _():
        for j in range(NR):
            relay(j).wait_send()

    for i in range(10):
        table(i).wait_send()


def per_device(s_blocks, s_list, x_blocks, x_list, c_list, owner):
    bs = s_blocks.shape[-1]
    smem = pl.BlockSpec(memory_space=pltpu.SMEM)
    vmem = pl.BlockSpec(memory_space=pltpu.VMEM)
    hbm = pl.BlockSpec(memory_space=pltpu.HBM)
    product = pl.pallas_call(
        kernel,
        out_shape=jax.ShapeDtypeStruct((NC, bs, bs), F32),
        in_specs=[smem, smem, vmem, vmem, hbm, hbm],
        out_specs=hbm,
        scratch_shapes=[
            *(pltpu.VMEM((4 * NS, tr, bs), F32) for tr in ROWS),
            *(pltpu.VMEM((RB * CB, tr, bs), F32) for tr in ROWS),
            pltpu.VMEM((HALF, bs, bs), F32),
            pltpu.VMEM((NX, bs, bs), F32),
            pltpu.VMEM((NX, bs, bs), F32),
            pltpu.VMEM((NX, bs, bs), F32),
            pltpu.VMEM((NX, bs, bs), F32),
            pltpu.VMEM((STEPS, CB, KB * bs, bs), BF16),
            pltpu.VMEM((STEPS, CB, KB * bs, bs), BF16),
            pltpu.VMEM((2, STEPS, 2 * RB * max(ROWS), KB * bs), BF16),
            pltpu.VMEM((NC, bs, bs), F32),
            pltpu.VMEM((KB * CB, 128), jnp.int32),
            pltpu.VMEM((8, KB * CB, 128), jnp.int32),
            pltpu.VMEM((4, KB * CB, 128), jnp.int32),
            pltpu.SMEM((8, KB * CB, 128), jnp.int32),
            pltpu.SMEM((4, KB * CB, 128), jnp.int32),
            pltpu.SemaphoreType.DMA((NT, 10)),
            pltpu.SemaphoreType.DMA((NT, 10)),
            pltpu.SemaphoreType.DMA((2,)),
            pltpu.SemaphoreType.DMA((2,)),
            pltpu.SemaphoreType.DMA((ND,)),
            pltpu.SemaphoreType.DMA((ND,)),
            pltpu.SemaphoreType.DMA((3, NR)),
            pltpu.SemaphoreType.DMA((3, NR)),
            pltpu.SemaphoreType.DMA((10,)),
            pltpu.SemaphoreType.DMA((10,)),
            pltpu.SemaphoreType.DMA((NT,)),
            pltpu.SemaphoreType.DMA((5,)),
            pltpu.SemaphoreType.DMA((NT,)),
        ],
        compiler_params=pltpu.CompilerParams(
            collective_id=0, has_side_effects=True, vmem_limit_bytes=60 * 1024 * 1024
        ),
        cost_estimate=pl.CostEstimate(flops=20 * 10**9, bytes_accessed=10**7, transcendentals=0),
    )(c_list[0, 0].T, owner, s_list[0, 0, 0].T, x_list[0, 0].T, s_blocks[0, 0, 0], x_blocks[0, 0])
    return product[None, None]


def solution(mesh):
    return jax.shard_map(
        per_device,
        mesh=mesh,
        in_specs=(
            P("loop", "bcast", None, None, None, None),
            P("loop", "bcast", None, None, None),
            P("loop", "bcast", None, None, None),
            P("loop", "bcast", None, None),
            P("loop", "bcast", None, None),
            P("loop", None),
        ),
        out_specs=P("loop", "bcast", None, None, None),
        check_vma=False,
    )
```

```python
import jax
import jax.numpy as jnp
from jax import lax
from jax.experimental import pallas as pl
from jax.experimental.pallas import tpu as pltpu
from jax.sharding import PartitionSpec as P

RB = 3
KB = 4
CB = 4
STEPS = 4
NS = 10
NX = 12
NC = 10
ROWS = (64, 80, 64, 48)
NT = len(ROWS)
STARTS = tuple(sum(ROWS[:t]) for t in range(NT))
ND = 6
NR = 3
HALF = NS // 2
MESH = pl.DeviceIdType.MESH
BF16 = jnp.bfloat16
F32 = jnp.float32


def kernel(c_s, owner_s, s_places, x_places, s_hbm, x_hbm, o_hbm, *rest):
    lbufs, accs = rest[:NT], rest[NT : 2 * NT]
    (recv1, r_own, r_a, r_two, r_b, rd_hi, rd_lo, l_dense, out_v, meta_v, group_v, density_v,
     group_s, density_s, ss, rs, rss, rrs, dss, drs, pss, prs, ms, mr, own_sem, local_sem, out_sem) = rest[2 * NT :]
    bs = s_hbm.shape[-1]
    n_loop, n_bcast = lax.axis_size("loop"), lax.axis_size("bcast")
    l, b = lax.axis_index("loop"), lax.axis_index("bcast")
    core = lax.rem(l, 2)
    hi_x = lax.rem(l // 2, 2)
    half = b // 4

    def loop_at(by):
        return (lax.rem(l + by + n_loop, n_loop), b)

    def bcast_at(by):
        return (l, lax.rem(b + by + n_bcast, n_bcast))

    def crossed(dev):
        return dev + 1 - 2 * lax.rem(dev, 2)

    def slot(dev):
        return 2 * lax.rem(dev, 4) + dev // 4

    across = (l, crossed(b))
    up, down = bcast_at(2), bcast_at(-2)
    sibling = (l + 1 - 2 * core, b)

    def stands(places, columns, count):
        cell = places[0:1, :] * columns + places[1:2, :]
        position = lax.broadcasted_iota(jnp.int32, (KB * CB, count), 0)
        entry = lax.broadcasted_iota(jnp.int32, (KB * CB, count), 1)
        return jnp.min(jnp.where(cell == position, entry, count), axis=1, keepdims=True)

    lane = lax.broadcasted_iota(jnp.int32, (KB * CB, 128), 1)
    meta_v[...] = jnp.where(lane == 0, stands(s_places, KB, NS), stands(x_places, CB, NX))

    barrier = pltpu.get_barrier_semaphore()
    peers = [bcast_at(i) for i in range(1, 8)] + [loop_at(i) for i in (-3, -2, -1, 1, 2, 3)]
    for peer in peers:
        pl.semaphore_signal(barrier, inc=1, device_id=peer, device_id_type=MESH)
    pl.semaphore_wait(barrier, len(peers))

    def remote(src, dst, send_sem, recv_sem, dev):
        return pltpu.make_async_remote_copy(
            src_ref=src, dst_ref=dst, send_sem=send_sem, recv_sem=recv_sem, device_id=dev, device_id_type=MESH
        )

    def whole(t, dev):
        return lbufs[t].at[pl.ds(HALF * slot(dev), HALF)]

    def part(t, dev, j):
        return lbufs[t].at[pl.ds(HALF * slot(dev), HALF), pl.ds(j * (ROWS[t] // 2), ROWS[t] // 2)]

    left, right = down[1], up[1]

    def margin(t, kind):
        if kind == 0:
            rows = pl.ds(STARTS[t], ROWS[t])
            src = s_hbm.at[pl.ds(HALF * (1 - half), HALF), rows]
            return remote(src, recv1.at[:, rows], ss.at[t, 0], rs.at[t, 0], bcast_at(4))
        ref, dev = {
            1: (lambda: whole(t, b), across),
            2: (lambda: whole(t, b), up),
            3: (lambda: whole(t, b), down),
            4: (lambda: whole(t, across[1]), up),
            5: (lambda: whole(t, across[1]), down),
            6: (lambda: part(t, left, 0), up),
            7: (lambda: part(t, right, 1), down),
            8: (lambda: part(t, crossed(left), 0), up),
            9: (lambda: part(t, crossed(right), 1), down),
        }[kind]
        return remote(ref(), ref(), ss.at[t, kind], rs.at[t, kind], dev)

    xn = NX // NR

    lower = (lax.rem(l - 3 + 2 * core + n_loop, n_loop), b)

    def density(kind):
        dev, src, dst = {
            1: (lower, x_hbm, r_a),
        }[kind]
        return remote(src, dst, rss.at[kind], rrs.at[kind], dev)

    def shared(j):
        at = pl.ds(j * xn, xn)
        return remote(r_two.at[at], r_b.at[at], pss.at[2, j], prs.at[2, j], sibling)

    def direct(k):
        at = pl.ds(k * (NX // ND), NX // ND)
        return remote(x_hbm.at[at], r_two.at[at], dss.at[k], drs.at[k], loop_at(-2))

    def relayed(j):
        at = pl.ds(j * xn, xn)
        return remote(x_hbm.at[at], r_a.at[at], pss.at[0, j], prs.at[0, j], lower)

    def relay(j):
        at = pl.ds(j * xn, xn)
        return remote(r_a.at[at], r_two.at[at], pss.at[1, j], prs.at[1, j], loop_at(1))

    gives = jnp.logical_and(hi_x == 0, core == 0)
    relays = jnp.logical_and(hi_x == 0, core == 1)
    takes = jnp.logical_and(hi_x == 1, core == 0)

    def either(flag, then, otherwise):
        pl.when(flag)(then)
        pl.when(jnp.logical_not(flag))(otherwise)

    def own_half(t):
        src = s_hbm.at[pl.ds(HALF * half, HALF), pl.ds(STARTS[t], ROWS[t])]
        return pltpu.make_async_copy(src, whole(t, b), own_sem.at[t])

    def begin(t):
        margin(t, 0).start()
        own_half(t).start()

    def table(i):
        if i < 7:
            return remote(meta_v, group_v.at[b], ms.at[i], mr.at[i], bcast_at(i + 1))
        by = i - 6
        return remote(meta_v, density_v.at[by], ms.at[i], mr.at[i], loop_at(-by))

    begin(0)
    begin(1)
    for i in range(10):
        table(i).start()
    mine_g = pltpu.make_async_copy(meta_v, group_v.at[b], local_sem.at[1])
    mine_d = pltpu.make_async_copy(meta_v, density_v.at[0], local_sem.at[2])
    mine_g.start()
    mine_d.start()

    either(gives, lambda: relayed(0).start(), lambda: density(1).start())

    @pl.when(jnp.logical_not(gives))
    def _():
        direct(0).start()
        direct(1).start()

    own_density = pltpu.make_async_copy(x_hbm, r_own, local_sem.at[0])
    own_density.start()

    def split(block):
        high = block.astype(BF16)
        return high, (block - high.astype(F32)).astype(BF16)

    def spread_density(ref, j, step):
        def body(i, carry):
            k, c = i // CB, lax.rem(i, CB)
            at = density_s[step, i, 1]
            block = jnp.where(at < NX, ref[jnp.minimum(at, NX - 1)], 0.0)
            rows = pl.ds(pl.multiple_of(k * bs, bs), bs)
            high, low = split(block)
            rd_hi[j, c, rows, :] = high
            rd_lo[j, c, rows, :] = low
            return carry

        lax.fori_loop(0, KB * CB, body, 0, unroll=2)

    wanted = (owner_s[0, 0] == b) | (owner_s[0, 1] == b) | (owner_s[0, 2] == b) | (owner_s[0, 3] == b)

    def choose(t):
        margin(t, 0).wait_recv()
        own_half(t).wait()

        def body(i, carry):
            at = HALF * slot(b) + i
            lbufs[t][at] = jnp.where(wanted, lbufs[t][at], recv1[i, STARTS[t] : STARTS[t] + ROWS[t], :])
            return carry

        lax.fori_loop(0, HALF, body, 0)
        for kind in (1, 2, 3):
            margin(t, kind).start()

    def cross(t):
        margin(t, 1).wait_recv()
        for kind in (4, 5):
            margin(t, kind).start()

    def forward_own(t):
        for kind in (2, 3):
            margin(t, kind).wait_recv()
            margin(t, kind + 4).start()

    def forward_crossed(t):
        for kind in (4, 5):
            margin(t, kind).wait_recv()
            margin(t, kind + 4).start()

    def finish(t):
        for kind in (6, 7, 8, 9):
            margin(t, kind).wait_recv()

    def advance(k):
        @pl.when(jnp.logical_not(gives))
        def _():
            direct(k).wait_send()
            direct(k + 2).start()

    def share(j):
        each = ND // NR

        def direct_in():
            for k in range(each * j, each * (j + 1)):
                direct(k).wait_recv()

        either(takes, lambda: relay(j).wait_recv(), direct_in)
        shared(j).start()

    def density_turn(j):
        if j + 1 < NR:

            @pl.when(gives)
            def _():
                relayed(j).wait_send()
                relayed(j + 1).start()

        @pl.when(relays)
        def _():
            relayed(j).wait_recv()
            relay(j).start()

    step_of = (0, 1 + 2 * core, 2, 3 - 2 * core)

    def spread_margin(t):
        for j in range(STEPS):
            root, tr = owner_s[0, step_of[j]], ROWS[t]

            def body(i, carry):
                r, k = i // KB, lax.rem(i, KB)
                at = group_s[root, i, 0]
                block = lbufs[t][NS * lax.rem(root, 4) + jnp.minimum(at, NS - 1)]
                high, low = split(jnp.where(at < NS, block, 0.0))
                cols = pl.ds(pl.multiple_of(k * bs, bs), bs)
                l_dense[t % 2, j, pl.ds(pl.multiple_of(r * tr, tr), tr), cols] = high
                l_dense[t % 2, j, pl.ds(pl.multiple_of((RB + r) * tr, tr), tr), cols] = low
                return carry

            lax.fori_loop(0, RB * KB, body, 0, unroll=4)

    def multiply(t, terms):
        tr, acc = ROWS[t], accs[t]

        def column(c, carry):
            total = jnp.zeros((RB * tr, bs), F32)
            for j in terms:
                first = jnp.dot(l_dense[t % 2, j, : 2 * RB * tr, :], rd_hi[j, c], preferred_element_type=F32)
                second = jnp.dot(l_dense[t % 2, j, : RB * tr, :], rd_lo[j, c], preferred_element_type=F32)
                total = total + (first[: RB * tr] + (first[RB * tr :] + second))
            for r in range(RB):
                piece = total[r * tr : (r + 1) * tr]
                acc[r * CB + c] = piece if terms[0] == 0 else acc[r * CB + c] + piece
            return carry

        lax.fori_loop(0, CB, column, 0)

    def keep(t):
        def body(m, carry):
            out_v[m, STARTS[t] : STARTS[t] + ROWS[t], :] = accs[t][c_s[0, m] * CB + c_s[1, m]]
            return carry

        lax.fori_loop(0, NC, body, 0, unroll=5)
        out(t).start()

    def out(t):
        at = pl.ds(STARTS[t], ROWS[t])
        return pltpu.make_async_copy(out_v.at[:, at], o_hbm.at[:, at], out_sem.at[t])

    choose(0)
    begin(2)
    advance(0)
    choose(1)
    begin(3)
    cross(0)
    for i in range(10):
        table(i).wait_recv()
    mine_g.wait()
    mine_d.wait()
    to_s = [
        pltpu.make_async_copy(group_v, group_s, local_sem.at[3]),
        pltpu.make_async_copy(density_v, density_s, local_sem.at[4]),
    ]
    for copy in to_s:
        copy.start()
    density_turn(0)
    advance(1)
    forward_own(0)
    choose(2)
    cross(1)
    for copy in to_s:
        copy.wait()
    own_density.wait()
    spread_density(r_own, 0, 0)
    advance(2)
    forward_crossed(0)
    density_turn(1)
    forward_own(1)
    choose(3)
    cross(2)
    advance(3)
    forward_crossed(1)
    density_turn(2)
    share(0)
    forward_own(2)
    cross(3)
    finish(0)
    pl.when(jnp.logical_not(relays))(lambda: density(1).wait_recv())
    spread_density(r_a, 1, step_of[1])
    spread_margin(0)
    multiply(0, (0, 1))
    share(1)
    forward_crossed(2)
    forward_own(3)

    share(2)
    spread_density(r_two, 2, 2)
    finish(1)
    spread_margin(1)
    multiply(1, (0, 1))
    for j in range(NR):
        shared(j).wait_recv()
    spread_density(r_b, 3, step_of[3])
    multiply(0, (2, 3))
    keep(0)
    forward_crossed(3)
    multiply(1, (2, 3))
    keep(1)
    for t in range(2, NT):
        finish(t)
        spread_margin(t)
        multiply(t, (0, 1, 2, 3))
        keep(t)

    for t in range(NT):
        out(t).wait()
        for kind in range(10):
            margin(t, kind).wait_send()
    for j in range(NR):
        shared(j).wait_send()

    def sent():
        density(1).wait_send()
        for k in range(ND - 2, ND):
            direct(k).wait_send()

    either(gives, lambda: relayed(NR - 1).wait_send(), sent)

    @pl.when(relays)
    def _():
        for j in range(NR):
            relay(j).wait_send()

    for i in range(10):
        table(i).wait_send()


def per_device(s_blocks, s_list, x_blocks, x_list, c_list, owner):
    bs = s_blocks.shape[-1]
    smem = pl.BlockSpec(memory_space=pltpu.SMEM)
    vmem = pl.BlockSpec(memory_space=pltpu.VMEM)
    hbm = pl.BlockSpec(memory_space=pltpu.HBM)
    product = pl.pallas_call(
        kernel,
        out_shape=jax.ShapeDtypeStruct((NC, bs, bs), F32),
        in_specs=[smem, smem, vmem, vmem, hbm, hbm],
        out_specs=hbm,
        scratch_shapes=[
            *(pltpu.VMEM((4 * NS, tr, bs), F32) for tr in ROWS),
            *(pltpu.VMEM((RB * CB, tr, bs), F32) for tr in ROWS),
            pltpu.VMEM((HALF, bs, bs), F32),
            pltpu.VMEM((NX, bs, bs), F32),
            pltpu.VMEM((NX, bs, bs), F32),
            pltpu.VMEM((NX, bs, bs), F32),
            pltpu.VMEM((NX, bs, bs), F32),
            pltpu.VMEM((STEPS, CB, KB * bs, bs), BF16),
            pltpu.VMEM((STEPS, CB, KB * bs, bs), BF16),
            pltpu.VMEM((2, STEPS, 2 * RB * max(ROWS), KB * bs), BF16),
            pltpu.VMEM((NC, bs, bs), F32),
            pltpu.VMEM((KB * CB, 128), jnp.int32),
            pltpu.VMEM((8, KB * CB, 128), jnp.int32),
            pltpu.VMEM((4, KB * CB, 128), jnp.int32),
            pltpu.SMEM((8, KB * CB, 128), jnp.int32),
            pltpu.SMEM((4, KB * CB, 128), jnp.int32),
            pltpu.SemaphoreType.DMA((NT, 10)),
            pltpu.SemaphoreType.DMA((NT, 10)),
            pltpu.SemaphoreType.DMA((2,)),
            pltpu.SemaphoreType.DMA((2,)),
            pltpu.SemaphoreType.DMA((ND,)),
            pltpu.SemaphoreType.DMA((ND,)),
            pltpu.SemaphoreType.DMA((3, NR)),
            pltpu.SemaphoreType.DMA((3, NR)),
            pltpu.SemaphoreType.DMA((10,)),
            pltpu.SemaphoreType.DMA((10,)),
            pltpu.SemaphoreType.DMA((NT,)),
            pltpu.SemaphoreType.DMA((5,)),
            pltpu.SemaphoreType.DMA((NT,)),
        ],
        compiler_params=pltpu.CompilerParams(
            collective_id=0, has_side_effects=True, vmem_limit_bytes=60 * 1024 * 1024
        ),
        cost_estimate=pl.CostEstimate(flops=20 * 10**9, bytes_accessed=10**7, transcendentals=0),
    )(c_list[0, 0].T, owner, s_list[0, 0, 0].T, x_list[0, 0].T, s_blocks[0, 0, 0], x_blocks[0, 0])
    return product[None, None]


def solution(mesh):
    return jax.shard_map(
        per_device,
        mesh=mesh,
        in_specs=(
            P("loop", "bcast", None, None, None, None),
            P("loop", "bcast", None, None, None),
            P("loop", "bcast", None, None, None),
            P("loop", "bcast", None, None),
            P("loop", "bcast", None, None),
            P("loop", None),
        ),
        out_specs=P("loop", "bcast", None, None, None),
        check_vma=False,
    )
```
